32 devices in a mesh: groups: 2 (over y), seq: 4 (over z), fam: 2 (over x), head: 2 (over core).
Axes of the slice: x: 2, y: 2, z: 4, core: 2. Of those that a mesh axis runs over, the one named last changes fastest.
Arguments:
- blocks: bfloat16 [16, 4, 128, 768], P(('groups', 'seq', 'fam'), None, None, 'head'), parts along dimension 0, may hold values from -6 to 6
- cotangent: bfloat16 [16, 4, 128, 768], P(('groups', 'seq', 'fam'), None, None, 'head'), parts along dimension 0, may hold values from -6 to 6
- w_query: bfloat16 [768, 768], P(None, 'head'), may hold values from -0.21875 to 0.21875
- w_key: bfloat16 [768, 768], P(None, 'head'), may hold values from -0.21875 to 0.21875
- w_value: bfloat16 [768, 768], P(None, 'head'), may hold values from -0.21875 to 0.21875
- w_out: bfloat16 [768, 768], P(None, 'head'), may hold values from -0.21875 to 0.21875
- block_family: int32 [16], P('groups'), parts along dimension 0, may hold values from 0 to 3, as said below
- family_depth: int32 [8], P('groups'), parts along dimension 0, may hold values from 1 to 20, as said below
Outputs:
- layer_out: bfloat16 [16, 4, 128, 768], P(('groups', 'seq', 'fam'), None, None, 'head'), parts along dimension 0
- input_grad: bfloat16 [16, 4, 128, 768], P(('groups', 'seq', 'fam'), None, None, 'head'), parts along dimension 0
- weight_grad: float32 [1536, 2, 768], P(('groups', 'seq', 'fam'), None, 'head'), parts along dimension 0
The draws below stay inside these ranges and needn't reach their ends.
There are 2 independent parts, one for each index of `groups`. The reference program is written for one: setup_inputs(seed, part) draws one part's arguments, and reference() takes and returns one part's arrays. A program takes and returns all parts, laid end to end along the dimension named above; an argument that names none is the same for every part. Nothing has to cross between parts.
Inputs may be any that keep to these rules, and one draw needn't show every extreme that they name: `block_family`: family numbers never fall along the blocks, and each of the 4 families holds at least one block. `family_depth`: A family that holds n blocks has a depth above (n - 1) * 4 and at most n * 4; one family holds 5 blocks.
All inputs are finite; a program needn't handle non-finite values.
Results may differ from the reference program's by a relative error of at most 0.011.
Values may be sent and summed in bfloat16 or wider, within the bound.
A program may use at most 64 MiB of HBM per device.

```python
import jax
import jax.numpy as jnp
from jax import lax

D = 768
H = 12
C = 128
BR = 4
F = 4
NBLK = 8


def family_layout(key):
    big_family = jax.random.randint(jax.random.fold_in(key, 13), (), 0, F).astype(jnp.int32)
    big_count = NBLK // 2 + NBLK // 8
    rest = NBLK - big_count
    cut_points = jnp.sort(jax.random.permutation(jax.random.fold_in(key, 11), rest - 1)[:F - 2] + 1).astype(jnp.int32)
    bounds = jnp.concatenate([jnp.zeros((1,), jnp.int32), cut_points, jnp.full((1,), rest, jnp.int32)])
    others = (bounds[1:] - bounds[:-1]).astype(jnp.int32)
    family_number = jnp.arange(F, dtype=jnp.int32)
    below_index = jnp.clip(family_number, 0, F - 2)
    above_index = jnp.clip(family_number - 1, 0, F - 2)
    counts = jnp.where(family_number < big_family, others[below_index], jnp.where(family_number == big_family, big_count, others[above_index])).astype(jnp.int32)
    ends = jnp.cumsum(counts).astype(jnp.int32)
    block_number = jnp.arange(NBLK, dtype=jnp.int32)
    families = jnp.sum((block_number[:, None] >= ends[None, :F - 1]).astype(jnp.int32), axis=1).astype(jnp.int32)
    return (families, big_family)


def draw_block_family(key, part):
    families, big_family = family_layout(key)
    return families


def draw_family_depth(key, part):
    families, big_family = family_layout(key)
    key = jax.random.fold_in(key, 5)
    family_number = jnp.arange(F, dtype=jnp.int32)
    counted = jnp.sum((families[None, :] == family_number[:, None]).astype(jnp.int32), axis=1)
    extra_rows = jax.random.randint(key, (F,), 1, BR + 1).astype(jnp.int32)
    extra_rows = jnp.where(family_number == big_family, BR, extra_rows)
    return ((counted - 1) * BR + extra_rows).astype(jnp.int32)


def block_levels(rng, shape, pieces, smallest, largest):
    gain = 1.0
    for axis_at, blocks in pieces:
        steps = jax.random.uniform(jax.random.fold_in(jax.random.fold_in(rng, 6), axis_at), (blocks,), jnp.float32, smallest / len(pieces), largest / len(pieces))
        gain = gain * jnp.repeat(jnp.exp(steps), shape[axis_at] // blocks).reshape((-1,) + (1,) * (len(shape) - 1 - axis_at))
    return gain


def scatter_about(own_key, shape, width, limit, pieces=(), held_as=jnp.bfloat16):
    result = jax.random.normal(own_key, shape, jnp.float32) * width
    if len(pieces) > 0:
        result = block_levels(own_key, shape, pieces, -0.22, 0.18) * result
    return jnp.clip(result, min=-limit, max=limit).astype(held_as)


def setup_inputs(seed: int = 0, part: int = 0) -> dict:
    arg_keys = jax.random.split(jax.random.key(seed), 9)
    part_keys = jax.random.split(jax.random.fold_in(arg_keys[8], part), 9)
    blocks = scatter_about(part_keys[0], (NBLK, BR, C, D), 1.0, 6.0, ((0, 8), (3, 2)))
    cotangent = scatter_about(part_keys[1], (NBLK, BR, C, D), 1.0, 6.0, ((0, 8), (3, 2)))
    w_query = scatter_about(arg_keys[2], (D, D), D ** -0.5, 0.21875, ((1, 2),))
    w_key = scatter_about(arg_keys[3], (D, D), D ** -0.5, 0.21875, ((1, 2),))
    w_value = scatter_about(arg_keys[4], (D, D), D ** -0.5, 0.21875, ((1, 2),))
    w_out = scatter_about(arg_keys[5], (D, D), D ** -0.5, 0.21875, ((1, 2),))
    block_family = draw_block_family(jax.random.fold_in(jax.random.fold_in(arg_keys[8], part), 71), part)
    family_depth = draw_family_depth(jax.random.fold_in(jax.random.fold_in(arg_keys[8], part), 71), part)
    return {"blocks": blocks, "cotangent": cotangent, "w_query": w_query, "w_key": w_key, "w_value": w_value, "w_out": w_out, "block_family": block_family, "family_depth": family_depth}


def reference(blocks, cotangent, w_query, w_key, w_value, w_out, block_family, family_depth):
    head_size = D // H
    flat_tokens = blocks.reshape(-1, D)
    shape_five = (NBLK, BR, C, H, head_size)

    def project(weight):
        return jnp.dot(flat_tokens, weight, preferred_element_type=jnp.float32).astype(jnp.bfloat16)
    query_rows = project(w_query)
    key_rows = project(w_key)
    value_rows = project(w_value)
    query_f32 = query_rows.reshape(shape_five).astype(jnp.float32)
    key_f32 = key_rows.reshape(shape_five).astype(jnp.float32)
    value_f32 = value_rows.reshape(shape_five).astype(jnp.float32)
    family_first = lax.optimization_barrier(jnp.sum((block_family[None, :] < jnp.arange(F, dtype=jnp.int32)[:, None]).astype(jnp.int32), axis=1))
    block_rank = jnp.arange(NBLK, dtype=jnp.int32) - family_first[block_family]
    block_depth = family_depth[block_family]
    row_place = block_rank[:, None] * BR + jnp.arange(BR, dtype=jnp.int32)[None, :]
    row_mask = (row_place < block_depth[:, None]).astype(jnp.float32)
    logit_scale = 1.0 / (jnp.sqrt(jnp.float32(head_size)) * jnp.sqrt(family_depth.astype(jnp.float32)))
    masked_query = query_f32 * row_mask[:, :, None, None, None]
    partial_logits = jnp.einsum('brihd,brjhd->bhij', masked_query, key_f32)
    logits = jax.ops.segment_sum(partial_logits, block_family, num_segments=F) * logit_scale[:, None, None, None]
    expo = jnp.exp(logits)
    attention = expo / lax.optimization_barrier(jnp.sum(expo, axis=-1, keepdims=True))
    attention_b16 = attention.astype(jnp.bfloat16)
    block_attention = attention_b16.astype(jnp.float32)[block_family]
    mixed = jnp.einsum('bhij,brjhd->brihd', block_attention, value_f32).astype(jnp.bfloat16)
    layer_out = jnp.dot(mixed.reshape(-1, D), w_out, preferred_element_type=jnp.float32).astype(jnp.bfloat16)
    flat_cot = cotangent.reshape(-1, D)
    out_grad = lax.dot_general(flat_cot, w_out, (((1,), (1,)), ((), ())), preferred_element_type=jnp.float32).astype(jnp.bfloat16)
    out_grad_f32 = out_grad.reshape(shape_five).astype(jnp.float32)
    partial_grad = jnp.einsum('brihd,brjhd->bhij', out_grad_f32, value_f32)
    attn_grad = jax.ops.segment_sum(partial_grad, block_family, num_segments=F)
    centred = attn_grad - lax.optimization_barrier(jnp.sum(attention * attn_grad, axis=-1, keepdims=True))
    logit_grad = (logit_scale[:, None, None, None] * attention * centred).astype(jnp.bfloat16)
    block_grad = logit_grad.astype(jnp.float32)[block_family]
    mask_five = row_mask[:, :, None, None, None]
    query_grad = (jnp.einsum('bhij,brjhd->brihd', block_grad, key_f32) * mask_five).astype(jnp.bfloat16)
    key_grad = (jnp.einsum('bhij,brihd->brjhd', block_grad, query_f32) * mask_five).astype(jnp.bfloat16)
    value_grad = jnp.einsum('bhij,brihd->brjhd', block_attention, out_grad_f32).astype(jnp.bfloat16)

    def back(grad, weight):
        return lax.dot_general(grad.reshape(-1, D), weight, (((1,), (1,)), ((), ())), preferred_element_type=jnp.float32)
    input_grad = (back(query_grad, w_query) + back(key_grad, w_key) + back(value_grad, w_value)).astype(jnp.bfloat16)
    grad_query_w = jnp.dot(flat_tokens.T, query_grad.reshape(-1, D), preferred_element_type=jnp.float32)
    grad_key_w = jnp.dot(flat_tokens.T, key_grad.reshape(-1, D), preferred_element_type=jnp.float32)
    weight_grad = jnp.stack([grad_query_w, grad_key_w], axis=1)
    return (layer_out.reshape(blocks.shape), input_grad.reshape(blocks.shape), weight_grad)
```

```python
import functools

import jax
import jax.numpy as jnp
from jax import lax
from jax.experimental import pallas as pl
from jax.experimental.pallas import tpu as pltpu
from jax.sharding import PartitionSpec as P

D = 768
H = 12
MESH = pl.DeviceIdType.MESH
F32 = jnp.float32
BF16 = jnp.bfloat16


def dot(a, b, ca=1, cb=0):
    return lax.dot_general(a, b, (((ca,), (cb,)), ((), ())), preferred_element_type=F32)


def kernel(cfg, fam_ref, depth_ref, x_ref, cot_ref, wq_ref, wk_ref, wv_ref, wo_ref,
           out_ref, ig_ref, wg_ref,
           xf, cf, wor, mf, igr, igs, qs, ks, vs, os_, kp, vp, gqk, gv,
           part, xrecv, lrecv, rrecv, fsend, bsend, tsend, tfull, gpart, gxrecv, gfrecv, gbrecv, gfsend, gbsend,
           h_send, h_recv, x_send, x_recv, f_send, f_recv, b_send, b_recv, t_send, t_recv,
           gx_send, gx_recv, gf_send, gf_recv, gb_send, gb_recv):
    n_seq, n_fam, rows, cols, own_rows, fused = cfg
    width = x_ref.shape[1]
    n_pairs = width // 128
    head_size = D // H
    chunk = 256 // n_fam
    n_blocks = n_seq * n_fam
    steps = 2 * n_pairs
    z = lax.axis_index("seq")
    x = lax.axis_index("fam")
    h = lax.axis_index("head")
    other = 1 - h
    last = n_seq - 1

    def fam_at(d):
        return lax.rem(x + d + n_fam, n_fam)

    barrier = pltpu.get_barrier_semaphore()
    pl.semaphore_signal(barrier, inc=1, device_id={"head": other}, device_id_type=MESH)
    for d in range(1, n_fam):
        pl.semaphore_signal(barrier, inc=1, device_id={"fam": fam_at(d)}, device_id_type=MESH)

    @pl.when(z > 0)
    def _():
        pl.semaphore_signal(barrier, inc=1, device_id={"seq": z - 1}, device_id_type=MESH)

    @pl.when(z < last)
    def _():
        pl.semaphore_signal(barrier, inc=1, device_id={"seq": z + 1}, device_id_type=MESH)

    @pl.when(z == 0)
    def _():
        lrecv[...] = jnp.zeros_like(lrecv)
        if fused:
            gfrecv[...] = jnp.zeros_like(gfrecv)

    @pl.when(z == last)
    def _():
        rrecv[...] = jnp.zeros_like(rrecv)
        if fused:
            gbrecv[...] = jnp.zeros_like(gbrecv)

    pl.semaphore_wait(barrier, n_fam + jnp.where(z > 0, 1, 0) + jnp.where(z < last, 1, 0))

    mine = pl.ds(pl.multiple_of(h * width, 128), width)
    theirs = pl.ds(pl.multiple_of(other * width, 128), width)

    def to_head(src, dst, k):
        return pltpu.make_async_remote_copy(
            src_ref=src, dst_ref=dst, send_sem=h_send.at[k], recv_sem=h_recv.at[k],
            device_id={"head": other}, device_id_type=MESH)

    cx = to_head(x_ref, xf.at[:, mine], 0)
    cx.start()
    cc = to_head(cot_ref, cf.at[:, mine], 1)
    cc.start()
    cw = to_head(wo_ref.at[theirs, :], wor.at[:, mine], 2)
    cw.start()
    xf[:, mine] = x_ref[...]
    cf[:, mine] = cot_ref[...]
    wor[:, mine] = wo_ref[mine, :]

    base = z * n_fam

    def family(b):
        return fam_ref[b]

    def same(a, b):
        return jnp.where(a == b, 1.0, 0.0).astype(F32)

    f_rel = [family(base + fam_at(d)) for d in range(n_fam)]
    f_neg = [family(base + fam_at(-d)) for d in range(n_fam)]
    f_first = family(base)
    f_last = family(base + n_fam - 1)
    has_left = jnp.where(z > 0, 1.0, 0.0).astype(F32)
    has_right = jnp.where(z < last, 1.0, 0.0).astype(F32)
    f_prev = family(base - jnp.where(z > 0, 1, 0))
    f_next = family(base + n_fam - 1 + jnp.where(z < last, 1, 0))
    my_family = f_rel[0]
    first = lax.fori_loop(
        0, n_blocks, lambda b, c: c + jnp.where(fam_ref[b] < my_family, 1, 0), jnp.int32(0))
    my_depth = depth_ref[my_family]
    rank = base + x - first
    live = [jnp.where(rank * rows + r < my_depth, 1.0, 0.0).astype(F32) for r in range(rows)]
    scale = []
    for d in range(n_fam):
        deep = jnp.full((8, 128), depth_ref[f_rel[d]].astype(F32), F32)
        scale.append((1.0 / (jnp.sqrt(jnp.full((8, 128), float(head_size), F32)) * jnp.sqrt(deep)))[0:1])

    low = lax.broadcasted_iota(jnp.int32, (cols, 128), 1) < head_size

    def keep(value, stack, plain, masked):
        for r in range(rows):
            for p in range(n_pairs):
                v = value[r * cols:(r + 1) * cols, p * 128:(p + 1) * 128]
                v = v.astype(BF16).astype(F32)
                if masked:
                    v = v * live[r]
                lanes = slice(r * 128, (r + 1) * 128)
                stack[p, 0:cols, lanes] = jnp.where(low, v, 0.0).astype(BF16)
                stack[p, cols:2 * cols, lanes] = jnp.where(low, 0.0, v).astype(BF16)
                if plain is not None:
                    plain[p, :, lanes] = v.astype(BF16)

    def x_copy(s, d):
        to = fam_at(d)
        return pltpu.make_async_remote_copy(
            src_ref=part.at[s, pl.ds(pl.multiple_of(to * chunk, 16), chunk)],
            dst_ref=xrecv.at[s, d], send_sem=x_send.at[s, d], recv_sem=x_recv.at[s, d],
            device_id={"fam": to}, device_id_type=MESH)

    cx.wait()
    keep(dot(xf[...], wq_ref[...]), qs, None, True)
    keep(dot(xf[...], wk_ref[...]), ks, kp, True)
    for p in range(n_pairs):
        part[p] = dot(qs[p], kp[p], 1, 1)
        for d in range(1, n_fam):
            x_copy(p, d).start()
    keep(dot(xf[...], wv_ref[...]), vs, vp, False)
    cc.wait()
    cw.wait()
    keep(dot(cf[...], wor[...], 1, 1), os_, None, False)
    for p in range(n_pairs):
        part[n_pairs + p] = dot(os_[p], vp[p], 1, 1)
        for d in range(1, n_fam):
            x_copy(n_pairs + p, d).start()

    own = pl.ds(pl.multiple_of(x * chunk, 16), chunk)

    def f_copy(s):
        return pltpu.make_async_remote_copy(
            src_ref=fsend.at[s], dst_ref=lrecv.at[s], send_sem=f_send.at[s], recv_sem=f_recv.at[s],
            device_id={"seq": z + 1}, device_id_type=MESH)

    def b_copy(s):
        return pltpu.make_async_remote_copy(
            src_ref=bsend.at[s], dst_ref=rrecv.at[s], send_sem=b_send.at[s], recv_sem=b_recv.at[s],
            device_id={"seq": z - 1}, device_id_type=MESH)

    def row_terms(s):
        return [part[s, own]] + [xrecv[s, d] for d in range(1, n_fam)]

    def chain(t, carry):
        sf = t - z
        sb = t - (last - z)

        @pl.when((sf >= 0) & (sf < steps))
        def _():
            @pl.when(z <= last - z)
            def _():
                for d in range(1, n_fam):
                    x_copy(sf, d).wait_recv()

            @pl.when(z > 0)
            def _():
                f_copy(sf).wait_recv()

            @pl.when(z < last)
            def _():
                total = (has_left * same(f_prev, f_last)) * lrecv[sf]
                for d, term in enumerate(row_terms(sf)):
                    total = total + same(f_neg[d], f_last) * term
                fsend[sf] = total
                f_copy(sf).start()

        @pl.when((sb >= 0) & (sb < steps))
        def _():
            @pl.when(z > last - z)
            def _():
                for d in range(1, n_fam):
                    x_copy(sb, d).wait_recv()

            @pl.when(z < last)
            def _():
                b_copy(sb).wait_recv()

            @pl.when(z > 0)
            def _():
                total = (has_right * same(f_next, f_first)) * rrecv[sb]
                for d, term in enumerate(row_terms(sb)):
                    total = total + same(f_neg[d], f_first) * term
                bsend[sb] = total
                b_copy(sb).start()

        return carry

    lax.fori_loop(0, steps + last, chain, jnp.int32(0))

    def t_copy(k, p, d):
        return pltpu.make_async_remote_copy(
            src_ref=tsend.at[k, p, d], dst_ref=tfull.at[k, p, own],
            send_sem=t_send.at[k, p, d], recv_sem=t_recv.at[k, p, d],
            device_id={"fam": fam_at(d)}, device_id_type=MESH)

    def t_wait(k, p, d):
        came = pl.ds(pl.multiple_of(fam_at(-d) * chunk, 16), chunk)
        pltpu.make_async_remote_copy(
            src_ref=tsend.at[k, p, d], dst_ref=tfull.at[k, p, came],
            send_sem=t_send.at[k, p, d], recv_sem=t_recv.at[k, p, d],
            device_id={"fam": fam_at(d)}, device_id_type=MESH).wait_recv()

    for p in range(n_pairs):
        sums = []
        for s in (p, n_pairs + p):
            terms = row_terms(s)
            left, right = lrecv[s], rrecv[s]
            for e in range(n_fam):
                total = (has_left * same(f_prev, f_rel[e])) * left
                total = total + (has_right * same(f_next, f_rel[e])) * right
                for d in range(n_fam):
                    total = total + same(f_neg[d], f_rel[e]) * terms[d]
                sums.append(total)
        for e in list(range(1, n_fam)) + [0]:
            expo = jnp.exp(sums[e] * scale[e])
            attention = expo / jnp.sum(expo, axis=-1, keepdims=True)
            grad = sums[n_fam + e]
            centred = grad - jnp.sum(attention * grad, axis=-1, keepdims=True)
            pair = (attention.astype(BF16), (scale[e] * attention * centred).astype(BF16))
            for k in (1, 0):
                if e == 0:
                    tfull[k, p, own] = pair[k]
                else:
                    tsend[k, p, e] = pair[k]
                    t_copy(k, p, e).start()

    def both(k, p):
        return jnp.concatenate([tfull[k, p, 0:cols], tfull[k, p, cols:2 * cols]], axis=1)

    def spread(value, ref, at):
        for r in range(rows):
            ref[r * cols:(r + 1) * cols, at:at + 128] = value[:, r * 128:(r + 1) * 128].astype(BF16)

    for p in range(n_pairs):
        for d in range(1, n_fam):
            t_wait(1, p, d)
        spread(dot(both(1, p), ks[p]), gqk, p * 128)
        spread(dot(tfull[1, p], qs[p], 0, 0), gqk, width + p * 128)

    for c in range(D // 256):
        piece = dot(xf[:, c * 256:(c + 1) * 256], gqk[...], 0, 0)
        if fused:
            gpart[c * 256:(c + 1) * 256] = piece.astype(BF16)
        else:
            wg_ref[c * 256:(c + 1) * 256] = piece

    def part_rows(to_z, to_x):
        return pl.ds(pl.multiple_of((to_z * n_fam + to_x) * own_rows, 16), own_rows)

    def gx_copy(to_z, d):
        return pltpu.make_async_remote_copy(
            src_ref=gpart.at[part_rows(to_z, fam_at(d))], dst_ref=gxrecv.at[to_z, d],
            send_sem=gx_send.at[to_z, d], recv_sem=gx_recv.at[to_z, d],
            device_id={"fam": fam_at(d)}, device_id_type=MESH)

    order = []
    for k in range(n_seq):
        order += [k // 2 if k % 2 == 0 else n_seq - 1 - k // 2]
    if fused:
        for to_z in order:
            for d in range(1, n_fam):
                gx_copy(to_z, d).start()

    for p in range(n_pairs):
        for d in range(1, n_fam):
            t_wait(0, p, d)
        mixed = dot(both(0, p), vs[p])
        for r in range(rows):
            mf[r * cols:(r + 1) * cols, pl.ds(pl.multiple_of(h * width + p * 128, 128), 128)] = (
                mixed[:, r * 128:(r + 1) * 128].astype(BF16))
    cm = to_head(mf.at[:, mine], mf.at[:, mine], 3)
    cm.start()
    for p in range(n_pairs):
        spread(dot(tfull[0, p], os_[p], 0, 0), gv, p * 128)

    def back(at):
        return (dot(gqk[:, 0:width], wq_ref[at, :], 1, 1)
                + dot(gqk[:, width:2 * width], wk_ref[at, :], 1, 1)
                + dot(gv[...], wv_ref[at, :], 1, 1))

    igs[...] = back(theirs).astype(igs.dtype)
    ci = to_head(igs, igr, 4)
    ci.start()
    cm.wait()
    out_ref[...] = dot(mf[...], wo_ref[...]).astype(BF16)
    mine_grad = back(mine)
    ci.wait()
    ig_ref[...] = (mine_grad + igr[...].astype(F32)).astype(BF16)

    if fused:
        for to_z in order:
            for d in range(1, n_fam):
                gx_copy(to_z, d).wait_recv()

        def g_term(to_z):
            total = gpart[part_rows(to_z, x)].astype(F32)
            for d in range(1, n_fam):
                total = total + gxrecv[to_z, d].astype(F32)
            return total

        def gf_copy(to_z):
            return pltpu.make_async_remote_copy(
                src_ref=gfsend.at[to_z], dst_ref=gfrecv.at[to_z],
                send_sem=gf_send.at[to_z], recv_sem=gf_recv.at[to_z],
                device_id={"seq": z + 1}, device_id_type=MESH)

        def gb_copy(to_z):
            return pltpu.make_async_remote_copy(
                src_ref=gbsend.at[to_z], dst_ref=gbrecv.at[to_z],
                send_sem=gb_send.at[to_z], recv_sem=gb_recv.at[to_z],
                device_id={"seq": z - 1}, device_id_type=MESH)

        def g_chain(t, carry):
            @pl.when(t >= z)
            def _():
                to_z = last - (t - z)

                @pl.when(z > 0)
                def _():
                    gf_copy(to_z).wait_recv()

                gfsend[to_z] = (g_term(to_z) + gfrecv[to_z].astype(F32)).astype(BF16)
                gf_copy(to_z).start()

            @pl.when(t >= last - z)
            def _():
                to_z = t - (last - z)

                @pl.when(z < last)
                def _():
                    gb_copy(to_z).wait_recv()

                gbsend[to_z] = (g_term(to_z) + gbrecv[to_z].astype(F32)).astype(BF16)
                gb_copy(to_z).start()

            return carry

        lax.fori_loop(0, last, g_chain, jnp.int32(0))

        @pl.when(z > 0)
        def _():
            gf_copy(z).wait_recv()

        @pl.when(z < last)
        def _():
            gb_copy(z).wait_recv()

        wg_ref[...] = g_term(z) + gfrecv[z].astype(F32) + gbrecv[z].astype(F32)

        def g_sent(t, carry):
            @pl.when(t >= z)
            def _():
                gf_copy(last - (t - z)).wait_send()

            @pl.when(t >= last - z)
            def _():
                gb_copy(t - (last - z)).wait_send()

            return carry

        lax.fori_loop(0, last, g_sent, jnp.int32(0))
        for to_z in order:
            for d in range(1, n_fam):
                gx_copy(to_z, d).wait_send()

    for s in range(steps):
        for d in range(1, n_fam):
            x_copy(s, d).wait_send()

        @pl.when(z < last)
        def _():
            f_copy(s).wait_send()

        @pl.when(z > 0)
        def _():
            b_copy(s).wait_send()
    for k in range(2):
        for p in range(n_pairs):
            for d in range(1, n_fam):
                t_copy(k, p, d).wait_send()


def shards(cfg, blocks, cotangent, w_query, w_key, w_value, w_out, block_family, family_depth):
    n_seq, n_fam, rows, cols, own_rows, fused = cfg
    tokens = rows * cols
    width = blocks.shape[3]
    n_pairs = width // 128
    steps = 2 * n_pairs
    chunk = 256 // n_fam
    lanes = rows * 128
    vmem = pltpu.VMEM
    dma = pltpu.SemaphoreType.DMA
    g_z, g_r = (n_seq, own_rows) if fused else (1, 16)
    g_all = D if fused else 16
    scratch = [
        vmem((tokens, D), BF16), vmem((tokens, D), BF16), vmem((width, D), BF16),
        vmem((tokens, D), BF16), vmem((tokens, width), BF16), vmem((tokens, width), BF16),
        vmem((n_pairs, 256, lanes), BF16), vmem((n_pairs, 256, lanes), BF16),
        vmem((n_pairs, 256, lanes), BF16), vmem((n_pairs, 256, lanes), BF16),
        vmem((n_pairs, 128, lanes), BF16), vmem((n_pairs, 128, lanes), BF16),
        vmem((tokens, 2 * width), BF16), vmem((tokens, width), BF16),
        vmem((steps, 256, 128), F32), vmem((steps, n_fam, chunk, 128), F32),
        vmem((steps, chunk, 128), F32), vmem((steps, chunk, 128), F32),
        vmem((steps, chunk, 128), F32), vmem((steps, chunk, 128), F32),
        vmem((2, n_pairs, n_fam, chunk, 128), BF16), vmem((2, n_pairs, 256, 128), BF16),
        vmem((g_all, 2 * width), BF16), vmem((g_z, n_fam, g_r, 2 * width), BF16),
        vmem((g_z, g_r, 2 * width), BF16), vmem((g_z, g_r, 2 * width), BF16),
        vmem((g_z, g_r, 2 * width), BF16), vmem((g_z, g_r, 2 * width), BF16),
        dma((5,)), dma((5,)), dma((steps, n_fam)), dma((steps, n_fam)),
        dma((steps,)), dma((steps,)), dma((steps,)), dma((steps,)),
        dma((2, n_pairs, n_fam)), dma((2, n_pairs, n_fam)),
        dma((g_z, n_fam)), dma((g_z, n_fam)), dma((g_z,)), dma((g_z,)), dma((g_z,)), dma((g_z,)),
    ]
    spec = pl.BlockSpec(memory_space=pltpu.VMEM)
    smem = pl.BlockSpec(memory_space=pltpu.SMEM)
    layer_out, input_grad, weight_grad = pl.pallas_call(
        functools.partial(kernel, cfg),
        out_shape=(
            jax.ShapeDtypeStruct((tokens, width), BF16),
            jax.ShapeDtypeStruct((tokens, width), BF16),
            jax.ShapeDtypeStruct((own_rows if fused else D, 2 * width), F32),
        ),
        in_specs=[smem, smem] + [spec] * 6,
        out_specs=(spec, spec, spec),
        scratch_shapes=scratch,
        compiler_params=pltpu.CompilerParams(
            collective_id=0, has_side_effects=True, vmem_limit_bytes=56 * 1024 * 1024),
    )(block_family, family_depth, blocks.reshape(tokens, width), cotangent.reshape(tokens, width),
      w_query, w_key, w_value, w_out)
    if not fused:
        weight_grad = lax.psum_scatter(weight_grad, ("seq", "fam"), scatter_dimension=0, tiled=True)
    return (
        layer_out.reshape(blocks.shape),
        input_grad.reshape(blocks.shape),
        weight_grad.reshape(own_rows, 2, width),
    )


def solution(mesh):
    n_seq, n_fam = mesh.shape["seq"], mesh.shape["fam"]

    def local(*arrays):
        own_rows = D // (n_seq * n_fam)
        blocks = arrays[0]
        rows = blocks.shape[0] * blocks.shape[1]
        cfg = (n_seq, n_fam, rows, blocks.shape[2], own_rows, own_rows % 16 == 0)
        return shards(cfg, *arrays)

    token_spec = P(("groups", "seq", "fam"), None, None, "head")
    weight_spec = P(None, "head")
    return jax.shard_map(
        local,
        mesh=mesh,
        in_specs=(token_spec, token_spec, weight_spec, weight_spec, weight_spec, weight_spec,
                  P("groups"), P("groups")),
        out_specs=(token_spec, token_spec, P(("groups", "seq", "fam"), None, "head")),
        check_vma=False,
    )
```

```python
import functools

import jax
import jax.numpy as jnp
from jax import lax
from jax.experimental import pallas as pl
from jax.experimental.pallas import tpu as pltpu
from jax.sharding import PartitionSpec as P

D = 768
H = 12
MESH = pl.DeviceIdType.MESH
F32 = jnp.float32
BF16 = jnp.bfloat16


def dot(a, b, ca=1, cb=0):
    return lax.dot_general(a, b, (((ca,), (cb,)), ((), ())), preferred_element_type=F32)


def kernel(cfg, fam_ref, depth_ref, x_ref, cot_ref, wq_ref, wk_ref, wv_ref, wo_ref,
           out_ref, ig_ref, wg_ref,
           xf, cf, wor, mf, igr, igs, qs, ks, vs, os_, kp, vp, gqk, gv,
           part, xrecv, lrecv, rrecv, fsend, bsend, tsend, tfull, gpart, gxrecv,
           qfrecv, qbrecv, qfsend, qbsend, kfrecv, kbrecv, kfsend, kbsend, kxsend, kxrecv,
           h_send, h_recv, x_send, x_recv, f_send, f_recv, b_send, b_recv, t_send, t_recv,
           gx_send, gx_recv, qf_send, qf_recv, qb_send, qb_recv,
           kf_send, kf_recv, kb_send, kb_recv, kx_send, kx_recv):
    n_seq, n_fam, rows, cols, own_rows, fused = cfg
    width = x_ref.shape[1]
    n_pairs = width // 128
    head_size = D // H
    chunk = 256 // n_fam
    n_blocks = n_seq * n_fam
    steps = 2 * n_pairs
    z = lax.axis_index("seq")
    x = lax.axis_index("fam")
    h = lax.axis_index("head")
    other = 1 - h
    last = n_seq - 1

    def fam_at(d):
        return lax.rem(x + d + n_fam, n_fam)

    barrier = pltpu.get_barrier_semaphore()
    pl.semaphore_signal(barrier, inc=1, device_id={"head": other}, device_id_type=MESH)
    for d in range(1, n_fam):
        pl.semaphore_signal(barrier, inc=1, device_id={"fam": fam_at(d)}, device_id_type=MESH)

    @pl.when(z > 0)
    def _():
        pl.semaphore_signal(barrier, inc=1, device_id={"seq": z - 1}, device_id_type=MESH)

    @pl.when(z < last)
    def _():
        pl.semaphore_signal(barrier, inc=1, device_id={"seq": z + 1}, device_id_type=MESH)

    @pl.when(z == 0)
    def _():
        lrecv[...] = jnp.zeros_like(lrecv)
        if fused:
            qfrecv[...] = jnp.zeros_like(qfrecv)
            kfrecv[...] = jnp.zeros_like(kfrecv)

    @pl.when(z == last)
    def _():
        rrecv[...] = jnp.zeros_like(rrecv)
        if fused:
            qbrecv[...] = jnp.zeros_like(qbrecv)
            kbrecv[...] = jnp.zeros_like(kbrecv)

    pl.semaphore_wait(barrier, n_fam + jnp.where(z > 0, 1, 0) + jnp.where(z < last, 1, 0))

    mine = pl.ds(pl.multiple_of(h * width, 128), width)
    theirs = pl.ds(pl.multiple_of(other * width, 128), width)

    def to_head(src, dst, k):
        return pltpu.make_async_remote_copy(
            src_ref=src, dst_ref=dst, send_sem=h_send.at[k], recv_sem=h_recv.at[k],
            device_id={"head": other}, device_id_type=MESH)

    cx = to_head(x_ref, xf.at[:, mine], 0)
    cx.start()
    cc = to_head(cot_ref, cf.at[:, mine], 1)
    cc.start()
    cw = to_head(wo_ref.at[theirs, :], wor.at[:, mine], 2)
    cw.start()
    xf[:, mine] = x_ref[...]
    cf[:, mine] = cot_ref[...]
    wor[:, mine] = wo_ref[mine, :]

    base = z * n_fam

    def family(b):
        return fam_ref[b]

    def same(a, b):
        return jnp.where(a == b, 1.0, 0.0).astype(F32)

    f_rel = [family(base + fam_at(d)) for d in range(n_fam)]
    f_neg = [family(base + fam_at(-d)) for d in range(n_fam)]
    f_first = family(base)
    f_last = family(base + n_fam - 1)
    has_left = jnp.where(z > 0, 1.0, 0.0).astype(F32)
    has_right = jnp.where(z < last, 1.0, 0.0).astype(F32)
    f_prev = family(base - jnp.where(z > 0, 1, 0))
    f_next = family(base + n_fam - 1 + jnp.where(z < last, 1, 0))
    my_family = f_rel[0]
    first = lax.fori_loop(
        0, n_blocks, lambda b, c: c + jnp.where(fam_ref[b] < my_family, 1, 0), jnp.int32(0))
    my_depth = depth_ref[my_family]
    rank = base + x - first
    live = [jnp.where(rank * rows + r < my_depth, 1.0, 0.0).astype(F32) for r in range(rows)]
    scale = []
    for d in range(n_fam):
        deep = jnp.full((8, 128), depth_ref[f_rel[d]].astype(F32), F32)
        scale.append((1.0 / (jnp.sqrt(jnp.full((8, 128), float(head_size), F32)) * jnp.sqrt(deep)))[0:1])

    low = lax.broadcasted_iota(jnp.int32, (cols, 128), 1) < head_size

    def keep(value, stack, plain, masked):
        for r in range(rows):
            for p in range(n_pairs):
                v = value[r * cols:(r + 1) * cols, p * 128:(p + 1) * 128]
                v = v.astype(BF16).astype(F32)
                if masked:
                    v = v * live[r]
                lanes = slice(r * 128, (r + 1) * 128)
                stack[p, 0:cols, lanes] = jnp.where(low, v, 0.0).astype(BF16)
                stack[p, cols:2 * cols, lanes] = jnp.where(low, 0.0, v).astype(BF16)
                if plain is not None:
                    plain[p, :, lanes] = v.astype(BF16)

    def x_copy(s, d):
        to = fam_at(d)
        return pltpu.make_async_remote_copy(
            src_ref=part.at[s, pl.ds(pl.multiple_of(to * chunk, 16), chunk)],
            dst_ref=xrecv.at[s, d], send_sem=x_send.at[s, d], recv_sem=x_recv.at[s, d],
            device_id={"fam": to}, device_id_type=MESH)

    cx.wait()
    keep(dot(xf[...], wq_ref[...]), qs, None, True)
    keep(dot(xf[...], wk_ref[...]), ks, kp, True)
    for p in range(n_pairs):
        part[p] = dot(qs[p], kp[p], 1, 1)
        for d in range(1, n_fam):
            x_copy(p, d).start()
    keep(dot(xf[...], wv_ref[...]), vs, vp, False)
    cc.wait()
    cw.wait()
    keep(dot(cf[...], wor[...], 1, 1), os_, None, False)
    for p in range(n_pairs):
        part[n_pairs + p] = dot(os_[p], vp[p], 1, 1)
        for d in range(1, n_fam):
            x_copy(n_pairs + p, d).start()

    own = pl.ds(pl.multiple_of(x * chunk, 16), chunk)

    def f_copy(s):
        return pltpu.make_async_remote_copy(
            src_ref=fsend.at[s], dst_ref=lrecv.at[s], send_sem=f_send.at[s], recv_sem=f_recv.at[s],
            device_id={"seq": z + 1}, device_id_type=MESH)

    def b_copy(s):
        return pltpu.make_async_remote_copy(
            src_ref=bsend.at[s], dst_ref=rrecv.at[s], send_sem=b_send.at[s], recv_sem=b_recv.at[s],
            device_id={"seq": z - 1}, device_id_type=MESH)

    def row_terms(s):
        return [part[s, own]] + [xrecv[s, d] for d in range(1, n_fam)]

    def chain(t, carry):
        sf = t - z
        sb = t - (last - z)

        @pl.when((sf >= 0) & (sf < steps))
        def _():
            @pl.when(z <= last - z)
            def _():
                for d in range(1, n_fam):
                    x_copy(sf, d).wait_recv()

            @pl.when(z > 0)
            def _():
                f_copy(sf).wait_recv()

            @pl.when(z < last)
            def _():
                total = (has_left * same(f_prev, f_last)) * lrecv[sf]
                for d, term in enumerate(row_terms(sf)):
                    total = total + same(f_neg[d], f_last) * term
                fsend[sf] = total
                f_copy(sf).start()

        @pl.when((sb >= 0) & (sb < steps))
        def _():
            @pl.when(z > last - z)
            def _():
                for d in range(1, n_fam):
                    x_copy(sb, d).wait_recv()

            @pl.when(z < last)
            def _():
                b_copy(sb).wait_recv()

            @pl.when(z > 0)
            def _():
                total = (has_right * same(f_next, f_first)) * rrecv[sb]
                for d, term in enumerate(row_terms(sb)):
                    total = total + same(f_neg[d], f_first) * term
                bsend[sb] = total
                b_copy(sb).start()

        return carry

    lax.fori_loop(0, steps + last, chain, jnp.int32(0))

    def t_copy(k, p, d):
        return pltpu.make_async_remote_copy(
            src_ref=tsend.at[k, p, d], dst_ref=tfull.at[k, p, own],
            send_sem=t_send.at[k, p, d], recv_sem=t_recv.at[k, p, d],
            device_id={"fam": fam_at(d)}, device_id_type=MESH)

    def t_wait(k, p, d):
        came = pl.ds(pl.multiple_of(fam_at(-d) * chunk, 16), chunk)
        pltpu.make_async_remote_copy(
            src_ref=tsend.at[k, p, d], dst_ref=tfull.at[k, p, came],
            send_sem=t_send.at[k, p, d], recv_sem=t_recv.at[k, p, d],
            device_id={"fam": fam_at(d)}, device_id_type=MESH).wait_recv()

    for p in range(n_pairs):
        sums = []
        for s in (p, n_pairs + p):
            terms = row_terms(s)
            left, right = lrecv[s], rrecv[s]
            for e in range(n_fam):
                total = (has_left * same(f_prev, f_rel[e])) * left
                total = total + (has_right * same(f_next, f_rel[e])) * right
                for d in range(n_fam):
                    total = total + same(f_neg[d], f_rel[e]) * terms[d]
                sums.append(total)
        for e in list(range(1, n_fam)) + [0]:
            expo = jnp.exp(sums[e] * scale[e])
            attention = expo / jnp.sum(expo, axis=-1, keepdims=True)
            grad = sums[n_fam + e]
            centred = grad - jnp.sum(attention * grad, axis=-1, keepdims=True)
            pair = (attention.astype(BF16), (scale[e] * attention * centred).astype(BF16))
            for k in (1, 0):
                if e == 0:
                    tfull[k, p, own] = pair[k]
                else:
                    tsend[k, p, e] = pair[k]
                    t_copy(k, p, e).start()

    def both(k, p):
        return jnp.concatenate([tfull[k, p, 0:cols], tfull[k, p, cols:2 * cols]], axis=1)

    def spread(value, ref, at):
        for r in range(rows):
            ref[r * cols:(r + 1) * cols, at:at + 128] = value[:, r * 128:(r + 1) * 128].astype(BF16)

    def part_rows(to_z, to_x, count):
        return pl.ds(pl.multiple_of((to_z * n_fam + to_x) * own_rows, 16), count)

    def gx_copy(to_z, d):
        return pltpu.make_async_remote_copy(
            src_ref=gpart.at[0, part_rows(to_z, fam_at(d), own_rows)], dst_ref=gxrecv.at[to_z, d],
            send_sem=gx_send.at[to_z, d], recv_sem=gx_recv.at[to_z, d],
            device_id={"fam": fam_at(d)}, device_id_type=MESH)

    def kx_copy(d):
        return pltpu.make_async_remote_copy(
            src_ref=kxsend.at[fam_at(d)], dst_ref=kxrecv.at[d], send_sem=kx_send.at[d], recv_sem=kx_recv.at[d],
            device_id={"fam": fam_at(d)}, device_id_type=MESH)

    def q_term(to_z):
        total = gpart[0, part_rows(to_z, x, own_rows)].astype(F32)
        for d in range(1, n_fam):
            gx_copy(to_z, d).wait_recv()
            total = total + gxrecv[to_z, d].astype(F32)
        return total

    def k_term(to_z):
        return gpart[1, part_rows(to_z, 0, n_fam * own_rows)].astype(F32)

    def two_way(term, fsrc, fdst, fs, fr, bsrc, bdst, bs, br):
        def fcopy(to_z):
            return pltpu.make_async_remote_copy(
                src_ref=fsrc.at[to_z], dst_ref=fdst.at[to_z], send_sem=fs.at[to_z], recv_sem=fr.at[to_z],
                device_id={"seq": z + 1}, device_id_type=MESH)

        def bcopy(to_z):
            return pltpu.make_async_remote_copy(
                src_ref=bsrc.at[to_z], dst_ref=bdst.at[to_z], send_sem=bs.at[to_z], recv_sem=br.at[to_z],
                device_id={"seq": z - 1}, device_id_type=MESH)

        def step(t):
            @pl.when(t >= z)
            def _():
                to_z = last - (t - z)
                total = term(to_z)

                @pl.when(z > 0)
                def _():
                    fcopy(to_z).wait_recv()

                fsrc[to_z] = (total + fdst[to_z].astype(F32)).astype(BF16)
                fcopy(to_z).start()

            @pl.when(t >= last - z)
            def _():
                to_z = t - (last - z)
                total = term(to_z)

                @pl.when(z < last)
                def _():
                    bcopy(to_z).wait_recv()

                bsrc[to_z] = (total + bdst[to_z].astype(F32)).astype(BF16)
                bcopy(to_z).start()

        def finish():
            total = term(z)

            @pl.when(z > 0)
            def _():
                fcopy(z).wait_recv()

            @pl.when(z < last)
            def _():
                bcopy(z).wait_recv()

            return total + fdst[z].astype(F32) + bdst[z].astype(F32)

        def sent():
            for t in range(last):
                @pl.when(t >= z)
                def _():
                    fcopy(last - (t - z)).wait_send()

                @pl.when(t >= last - z)
                def _():
                    bcopy(t - (last - z)).wait_send()

        def steps_of(lo, hi):
            if fused:
                for t in range(lo, min(hi, last)):
                    step(t)

        return steps_of, finish, sent

    q_steps, q_finish, q_sent = two_way(
        q_term, qfsend, qfrecv, qf_send, qf_recv, qbsend, qbrecv, qb_send, qb_recv)
    k_steps, k_finish, k_sent = two_way(
        k_term, kfsend, kfrecv, kf_send, kf_recv, kbsend, kbrecv, kb_send, kb_recv)

    def weight_part(k):
        for c in range(D // 256):
            piece = dot(xf[:, c * 256:(c + 1) * 256], gqk[:, k * width:(k + 1) * width], 0, 0)
            if fused:
                gpart[k, c * 256:(c + 1) * 256] = piece.astype(BF16)
            else:
                wg_ref[c * 256:(c + 1) * 256, k * width:(k + 1) * width] = piece

    for p in range(n_pairs):
        for d in range(1, n_fam):
            t_wait(1, p, d)
        spread(dot(tfull[1, p], qs[p], 0, 0), gqk, width + p * 128)
    weight_part(1)
    k_steps(0, 1)
    for p in range(n_pairs):
        spread(dot(both(1, p), ks[p]), gqk, p * 128)
    weight_part(0)
    order = []
    for k in range(n_seq):
        order += [k // 2 if k % 2 == 0 else n_seq - 1 - k // 2]
    if fused:
        for to_z in order:
            for d in range(1, n_fam):
                gx_copy(to_z, d).start()

    for p in range(n_pairs):
        for d in range(1, n_fam):
            t_wait(0, p, d)
        mixed = dot(both(0, p), vs[p])
        for r in range(rows):
            mf[r * cols:(r + 1) * cols, pl.ds(pl.multiple_of(h * width + p * 128, 128), 128)] = (
                mixed[:, r * 128:(r + 1) * 128].astype(BF16))
    cm = to_head(mf.at[:, mine], mf.at[:, mine], 3)
    cm.start()
    k_steps(1, 2)
    for p in range(n_pairs):
        spread(dot(tfull[0, p], os_[p], 0, 0), gv, p * 128)

    def back(at):
        return (dot(gqk[:, 0:width], wq_ref[at, :], 1, 1)
                + dot(gqk[:, width:2 * width], wk_ref[at, :], 1, 1)
                + dot(gv[...], wv_ref[at, :], 1, 1))

    q_steps(0, 1)
    igs[...] = back(theirs).astype(igs.dtype)
    ci = to_head(igs, igr, 4)
    ci.start()
    k_steps(2, last)
    q_steps(1, 2)
    if fused:
        summed = k_finish()
        kxsend[...] = summed.astype(BF16).reshape(n_fam, own_rows, width)
        for d in range(1, n_fam):
            kx_copy(d).start()
    cm.wait()
    out_ref[...] = dot(mf[...], wo_ref[...]).astype(BF16)
    q_steps(2, last)
    mine_grad = back(mine)
    ci.wait()
    ig_ref[...] = (mine_grad + igr[...].astype(F32)).astype(BF16)
    if fused:
        wg_ref[:, 0, :] = q_finish()
        total = kxsend[x].astype(F32)
        for d in range(1, n_fam):
            kx_copy(d).wait_recv()
            total = total + kxrecv[d].astype(F32)
        wg_ref[:, 1, :] = total
        q_sent()
        k_sent()
        for d in range(1, n_fam):
            kx_copy(d).wait_send()
        for to_z in order:
            for d in range(1, n_fam):
                gx_copy(to_z, d).wait_send()

    for s in range(steps):
        for d in range(1, n_fam):
            x_copy(s, d).wait_send()

        @pl.when(z < last)
        def _():
            f_copy(s).wait_send()

        @pl.when(z > 0)
        def _():
            b_copy(s).wait_send()
    for k in range(2):
        for p in range(n_pairs):
            for d in range(1, n_fam):
                t_copy(k, p, d).wait_send()


def shards(cfg, blocks, cotangent, w_query, w_key, w_value, w_out, block_family, family_depth):
    n_seq, n_fam, rows, cols, own_rows, fused = cfg
    tokens = rows * cols
    width = blocks.shape[3]
    n_pairs = width // 128
    steps = 2 * n_pairs
    chunk = 256 // n_fam
    lanes = rows * 128
    vmem = pltpu.VMEM
    dma = pltpu.SemaphoreType.DMA
    g_z, g_r = (n_seq, own_rows) if fused else (1, 16)
    g_all = D if fused else 16
    scratch = [
        vmem((tokens, D), BF16), vmem((tokens, D), BF16), vmem((width, D), BF16),
        vmem((tokens, D), BF16), vmem((tokens, width), BF16), vmem((tokens, width), BF16),
        vmem((n_pairs, 256, lanes), BF16), vmem((n_pairs, 256, lanes), BF16),
        vmem((n_pairs, 256, lanes), BF16), vmem((n_pairs, 256, lanes), BF16),
        vmem((n_pairs, 128, lanes), BF16), vmem((n_pairs, 128, lanes), BF16),
        vmem((tokens, 2 * width), BF16), vmem((tokens, width), BF16),
        vmem((steps, 256, 128), F32), vmem((steps, n_fam, chunk, 128), F32),
        vmem((steps, chunk, 128), F32), vmem((steps, chunk, 128), F32),
        vmem((steps, chunk, 128), F32), vmem((steps, chunk, 128), F32),
        vmem((2, n_pairs, n_fam, chunk, 128), BF16), vmem((2, n_pairs, 256, 128), BF16),
        vmem((2, g_all, width), BF16), vmem((g_z, n_fam, g_r, width), BF16),
        vmem((g_z, g_r, width), BF16), vmem((g_z, g_r, width), BF16),
        vmem((g_z, g_r, width), BF16), vmem((g_z, g_r, width), BF16),
        vmem((g_z, n_fam * g_r, width), BF16), vmem((g_z, n_fam * g_r, width), BF16),
        vmem((g_z, n_fam * g_r, width), BF16), vmem((g_z, n_fam * g_r, width), BF16),
        vmem((n_fam, g_r, width), BF16), vmem((n_fam, g_r, width), BF16),
        dma((5,)), dma((5,)), dma((steps, n_fam)), dma((steps, n_fam)),
        dma((steps,)), dma((steps,)), dma((steps,)), dma((steps,)),
        dma((2, n_pairs, n_fam)), dma((2, n_pairs, n_fam)),
        dma((g_z, n_fam)), dma((g_z, n_fam)), dma((g_z,)), dma((g_z,)), dma((g_z,)), dma((g_z,)),
        dma((g_z,)), dma((g_z,)), dma((g_z,)), dma((g_z,)), dma((n_fam,)), dma((n_fam,)),
    ]
    spec = pl.BlockSpec(memory_space=pltpu.VMEM)
    smem = pl.BlockSpec(memory_space=pltpu.SMEM)
    layer_out, input_grad, weight_grad = pl.pallas_call(
        functools.partial(kernel, cfg),
        out_shape=(
            jax.ShapeDtypeStruct((tokens, width), BF16),
            jax.ShapeDtypeStruct((tokens, width), BF16),
            jax.ShapeDtypeStruct((own_rows, 2, width) if fused else (D, 2 * width), F32),
        ),
        in_specs=[smem, smem] + [spec] * 6,
        out_specs=(spec, spec, spec),
        scratch_shapes=scratch,
        compiler_params=pltpu.CompilerParams(
            collective_id=0, has_side_effects=True, vmem_limit_bytes=56 * 1024 * 1024),
    )(block_family, family_depth, blocks.reshape(tokens, width), cotangent.reshape(tokens, width),
      w_query, w_key, w_value, w_out)
    if not fused:
        weight_grad = lax.psum_scatter(weight_grad, ("seq", "fam"), scatter_dimension=0, tiled=True)
    return (
        layer_out.reshape(blocks.shape),
        input_grad.reshape(blocks.shape),
        weight_grad.reshape(own_rows, 2, width),
    )


def solution(mesh):
    n_seq, n_fam = mesh.shape["seq"], mesh.shape["fam"]

    def local(*arrays):
        own_rows = D // (n_seq * n_fam)
        blocks = arrays[0]
        rows = blocks.shape[0] * blocks.shape[1]
        cfg = (n_seq, n_fam, rows, blocks.shape[2], own_rows, own_rows % 16 == 0)
        return shards(cfg, *arrays)

    token_spec = P(("groups", "seq", "fam"), None, None, "head")
    weight_spec = P(None, "head")
    return jax.shard_map(
        local,
        mesh=mesh,
        in_specs=(token_spec, token_spec, weight_spec, weight_spec, weight_spec, weight_spec,
                  P("groups"), P("groups")),
        out_specs=(token_spec, token_spec, P(("groups", "seq", "fam"), None, "head")),
        check_vma=False,
    )
```

```python
import functools

import jax
import jax.numpy as jnp
from jax import lax
from jax.experimental import pallas as pl
from jax.experimental.pallas import tpu as pltpu
from jax.sharding import PartitionSpec as P

D = 768
H = 12
MESH = pl.DeviceIdType.MESH
F32 = jnp.float32
BF16 = jnp.bfloat16


def dot(a, b, ca=1, cb=0):
    return lax.dot_general(a, b, (((ca,), (cb,)), ((), ())), preferred_element_type=F32)


def kernel(cfg, fam_ref, depth_ref, x_ref, cot_ref, wq_ref, wk_ref, wv_ref, wo_ref,
           out_ref, ig_ref, wg_ref,
           xf, cf, wor, mf, igr, igs, qs, ks, vs, os_, kp, vp, gqk, gv,
           part, xrecv, lrecv, rrecv, fsend, bsend, tsend, tfull, att, gpart, gxrecv,
           qfrecv, qbrecv, qfsend, qbsend, kfrecv, kbrecv, kfsend, kbsend, kxsend, kxrecv,
           h_send, h_recv, x_send, x_recv, f_send, f_recv, b_send, b_recv, t_send, t_recv,
           gx_send, gx_recv, qf_send, qf_recv, qb_send, qb_recv,
           kf_send, kf_recv, kb_send, kb_recv, kx_send, kx_recv):
    n_seq, n_fam, rows, cols, own_rows, fused = cfg
    width = x_ref.shape[1]
    n_pairs = width // 128
    head_size = D // H
    chunk = 256 // n_fam
    n_blocks = n_seq * n_fam
    steps = 2 * n_pairs
    z = lax.axis_index("seq")
    x = lax.axis_index("fam")
    h = lax.axis_index("head")
    other = 1 - h
    last = n_seq - 1

    def fam_at(d):
        return lax.rem(x + d + n_fam, n_fam)

    barrier = pltpu.get_barrier_semaphore()
    pl.semaphore_signal(barrier, inc=1, device_id={"head": other}, device_id_type=MESH)
    for d in range(1, n_fam):
        pl.semaphore_signal(barrier, inc=1, device_id={"fam": fam_at(d)}, device_id_type=MESH)

    @pl.when(z > 0)
    def _():
        pl.semaphore_signal(barrier, inc=1, device_id={"seq": z - 1}, device_id_type=MESH)

    @pl.when(z < last)
    def _():
        pl.semaphore_signal(barrier, inc=1, device_id={"seq": z + 1}, device_id_type=MESH)

    @pl.when(z == 0)
    def _():
        lrecv[...] = jnp.zeros_like(lrecv)
        if fused:
            qfrecv[...] = jnp.zeros_like(qfrecv)
            kfrecv[...] = jnp.zeros_like(kfrecv)

    @pl.when(z == last)
    def _():
        rrecv[...] = jnp.zeros_like(rrecv)
        if fused:
            qbrecv[...] = jnp.zeros_like(qbrecv)
            kbrecv[...] = jnp.zeros_like(kbrecv)

    pl.semaphore_wait(barrier, n_fam + jnp.where(z > 0, 1, 0) + jnp.where(z < last, 1, 0))

    mine = pl.ds(pl.multiple_of(h * width, 128), width)
    theirs = pl.ds(pl.multiple_of(other * width, 128), width)

    def to_head(src, dst, k):
        return pltpu.make_async_remote_copy(
            src_ref=src, dst_ref=dst, send_sem=h_send.at[k], recv_sem=h_recv.at[k],
            device_id={"head": other}, device_id_type=MESH)

    cx = to_head(x_ref, xf.at[:, mine], 0)
    cx.start()
    cc = to_head(cot_ref, cf.at[:, mine], 1)
    cc.start()
    cw = to_head(wo_ref.at[theirs, :], wor.at[:, mine], 2)
    cw.start()
    xf[:, mine] = x_ref[...]
    cf[:, mine] = cot_ref[...]
    wor[:, mine] = wo_ref[mine, :]

    base = z * n_fam

    def family(b):
        return fam_ref[b]

    def same(a, b):
        return jnp.where(a == b, 1.0, 0.0).astype(F32)

    f_rel = [family(base + fam_at(d)) for d in range(n_fam)]
    f_neg = [family(base + fam_at(-d)) for d in range(n_fam)]
    f_first = family(base)
    f_last = family(base + n_fam - 1)
    has_left = jnp.where(z > 0, 1.0, 0.0).astype(F32)
    has_right = jnp.where(z < last, 1.0, 0.0).astype(F32)
    f_prev = family(base - jnp.where(z > 0, 1, 0))
    f_next = family(base + n_fam - 1 + jnp.where(z < last, 1, 0))
    my_family = f_rel[0]
    first = lax.fori_loop(
        0, n_blocks, lambda b, c: c + jnp.where(fam_ref[b] < my_family, 1, 0), jnp.int32(0))
    my_depth = depth_ref[my_family]
    rank = base + x - first
    live = [jnp.where(rank * rows + r < my_depth, 1.0, 0.0).astype(F32) for r in range(rows)]
    scale = []
    for d in range(n_fam):
        deep = jnp.full((8, 128), depth_ref[f_rel[d]].astype(F32), F32)
        scale.append((1.0 / (jnp.sqrt(jnp.full((8, 128), float(head_size), F32)) * jnp.sqrt(deep)))[0:1])

    low = lax.broadcasted_iota(jnp.int32, (cols, 128), 1) < head_size

    def keep(value, stack, plain, masked):
        for r in range(rows):
            for p in range(n_pairs):
                v = value[r * cols:(r + 1) * cols, p * 128:(p + 1) * 128]
                v = v.astype(BF16).astype(F32)
                if masked:
                    v = v * live[r]
                lanes = slice(r * 128, (r + 1) * 128)
                stack[p, 0:cols, lanes] = jnp.where(low, v, 0.0).astype(BF16)
                stack[p, cols:2 * cols, lanes] = jnp.where(low, 0.0, v).astype(BF16)
                if plain is not None:
                    plain[p, :, lanes] = v.astype(BF16)

    def x_copy(s, d):
        to = fam_at(d)
        return pltpu.make_async_remote_copy(
            src_ref=part.at[s, pl.ds(pl.multiple_of(to * chunk, 16), chunk)],
            dst_ref=xrecv.at[s, d], send_sem=x_send.at[s, d], recv_sem=x_recv.at[s, d],
            device_id={"fam": to}, device_id_type=MESH)

    cx.wait()
    keep(dot(xf[...], wq_ref[...]), qs, None, True)
    keep(dot(xf[...], wk_ref[...]), ks, kp, True)
    for p in range(n_pairs):
        part[p] = dot(qs[p], kp[p], 1, 1)
        for d in range(1, n_fam):
            x_copy(p, d).start()
    keep(dot(xf[...], wv_ref[...]), vs, vp, False)
    cc.wait()
    cw.wait()
    keep(dot(cf[...], wor[...], 1, 1), os_, None, False)
    for p in range(n_pairs):
        part[n_pairs + p] = dot(os_[p], vp[p], 1, 1)
        for d in range(1, n_fam):
            x_copy(n_pairs + p, d).start()

    own = pl.ds(pl.multiple_of(x * chunk, 16), chunk)

    def f_copy(s):
        return pltpu.make_async_remote_copy(
            src_ref=fsend.at[s], dst_ref=lrecv.at[s], send_sem=f_send.at[s], recv_sem=f_recv.at[s],
            device_id={"seq": z + 1}, device_id_type=MESH)

    def b_copy(s):
        return pltpu.make_async_remote_copy(
            src_ref=bsend.at[s], dst_ref=rrecv.at[s], send_sem=b_send.at[s], recv_sem=b_recv.at[s],
            device_id={"seq": z - 1}, device_id_type=MESH)

    def row_terms(s):
        return [part[s, own]] + [xrecv[s, d] for d in range(1, n_fam)]

    def chain(t, carry):
        sf = t - z
        sb = t - (last - z)

        @pl.when((sf >= 0) & (sf < steps))
        def _():
            @pl.when(z <= last - z)
            def _():
                for d in range(1, n_fam):
                    x_copy(sf, d).wait_recv()

            @pl.when(z > 0)
            def _():
                f_copy(sf).wait_recv()

            @pl.when(z < last)
            def _():
                total = (has_left * same(f_prev, f_last)) * lrecv[sf]
                for d, term in enumerate(row_terms(sf)):
                    total = total + same(f_neg[d], f_last) * term
                fsend[sf] = total
                f_copy(sf).start()

        @pl.when((sb >= 0) & (sb < steps))
        def _():
            @pl.when(z > last - z)
            def _():
                for d in range(1, n_fam):
                    x_copy(sb, d).wait_recv()

            @pl.when(z < last)
            def _():
                b_copy(sb).wait_recv()

            @pl.when(z > 0)
            def _():
                total = (has_right * same(f_next, f_first)) * rrecv[sb]
                for d, term in enumerate(row_terms(sb)):
                    total = total + same(f_neg[d], f_first) * term
                bsend[sb] = total
                b_copy(sb).start()

        return carry

    logits_done = n_pairs + last
    lax.fori_loop(0, logits_done, chain, jnp.int32(0))

    def t_copy(k, p, d):
        return pltpu.make_async_remote_copy(
            src_ref=tsend.at[k, p, d], dst_ref=tfull.at[k, p, own],
            send_sem=t_send.at[k, p, d], recv_sem=t_recv.at[k, p, d],
            device_id={"fam": fam_at(d)}, device_id_type=MESH)

    def t_wait(k, p, d):
        came = pl.ds(pl.multiple_of(fam_at(-d) * chunk, 16), chunk)
        pltpu.make_async_remote_copy(
            src_ref=tsend.at[k, p, d], dst_ref=tfull.at[k, p, came],
            send_sem=t_send.at[k, p, d], recv_sem=t_recv.at[k, p, d],
            device_id={"fam": fam_at(d)}, device_id_type=MESH).wait_recv()

    def totals(s):
        terms = row_terms(s)
        left, right = lrecv[s], rrecv[s]
        sums = []
        for e in range(n_fam):
            total = (has_left * same(f_prev, f_rel[e])) * left
            total = total + (has_right * same(f_next, f_rel[e])) * right
            for d in range(n_fam):
                total = total + same(f_neg[d], f_rel[e]) * terms[d]
            sums.append(total)
        return sums

    def give(k, p, e, value):
        if e == 0:
            tfull[k, p, own] = value
        else:
            tsend[k, p, e] = value
            t_copy(k, p, e).start()

    for p in range(n_pairs):
        sums = totals(p)
        for e in list(range(1, n_fam)) + [0]:
            expo = jnp.exp(sums[e] * scale[e])
            attention = expo / jnp.sum(expo, axis=-1, keepdims=True)
            att[p, e] = attention
            give(0, p, e, attention.astype(BF16))
        if p < last:
            chain(logits_done + p, 0)
    for t in range(logits_done + min(n_pairs, last), steps + last):
        chain(t, 0)

    for p in range(n_pairs):
        sums = totals(n_pairs + p)
        for e in list(range(1, n_fam)) + [0]:
            attention, grad = att[p, e], sums[e]
            centred = grad - jnp.sum(attention * grad, axis=-1, keepdims=True)
            give(1, p, e, (scale[e] * attention * centred).astype(BF16))

    def both(k, p):
        return jnp.concatenate([tfull[k, p, 0:cols], tfull[k, p, cols:2 * cols]], axis=1)

    def spread(value, ref, at):
        for r in range(rows):
            ref[r * cols:(r + 1) * cols, at:at + 128] = value[:, r * 128:(r + 1) * 128].astype(BF16)

    def part_rows(to_z, to_x, count):
        return pl.ds(pl.multiple_of((to_z * n_fam + to_x) * own_rows, 16), count)

    def gx_copy(to_z, d):
        return pltpu.make_async_remote_copy(
            src_ref=gpart.at[0, part_rows(to_z, fam_at(d), own_rows)], dst_ref=gxrecv.at[to_z, d],
            send_sem=gx_send.at[to_z, d], recv_sem=gx_recv.at[to_z, d],
            device_id={"fam": fam_at(d)}, device_id_type=MESH)

    def kx_copy(d):
        return pltpu.make_async_remote_copy(
            src_ref=kxsend.at[fam_at(d)], dst_ref=kxrecv.at[d], send_sem=kx_send.at[d], recv_sem=kx_recv.at[d],
            device_id={"fam": fam_at(d)}, device_id_type=MESH)

    def q_term(to_z):
        total = gpart[0, part_rows(to_z, x, own_rows)].astype(F32)
        for d in range(1, n_fam):
            gx_copy(to_z, d).wait_recv()
            total = total + gxrecv[to_z, d].astype(F32)
        return total

    def k_term(to_z):
        return gpart[1, part_rows(to_z, 0, n_fam * own_rows)].astype(F32)

    def two_way(term, fsrc, fdst, fs, fr, bsrc, bdst, bs, br):
        def fcopy(to_z):
            return pltpu.make_async_remote_copy(
                src_ref=fsrc.at[to_z], dst_ref=fdst.at[to_z], send_sem=fs.at[to_z], recv_sem=fr.at[to_z],
                device_id={"seq": z + 1}, device_id_type=MESH)

        def bcopy(to_z):
            return pltpu.make_async_remote_copy(
                src_ref=bsrc.at[to_z], dst_ref=bdst.at[to_z], send_sem=bs.at[to_z], recv_sem=br.at[to_z],
                device_id={"seq": z - 1}, device_id_type=MESH)

        def step(t):
            @pl.when(t >= z)
            def _():
                to_z = last - (t - z)
                total = term(to_z)

                @pl.when(z > 0)
                def _():
                    fcopy(to_z).wait_recv()

                fsrc[to_z] = (total + fdst[to_z].astype(F32)).astype(BF16)
                fcopy(to_z).start()

            @pl.when(t >= last - z)
            def _():
                to_z = t - (last - z)
                total = term(to_z)

                @pl.when(z < last)
                def _():
                    bcopy(to_z).wait_recv()

                bsrc[to_z] = (total + bdst[to_z].astype(F32)).astype(BF16)
                bcopy(to_z).start()

        def finish():
            total = term(z)

            @pl.when(z > 0)
            def _():
                fcopy(z).wait_recv()

            @pl.when(z < last)
            def _():
                bcopy(z).wait_recv()

            return total + fdst[z].astype(F32) + bdst[z].astype(F32)

        def sent():
            for t in range(last):
                @pl.when(t >= z)
                def _():
                    fcopy(last - (t - z)).wait_send()

                @pl.when(t >= last - z)
                def _():
                    bcopy(t - (last - z)).wait_send()

        def steps_of(lo, hi):
            if fused:
                for t in range(lo, min(hi, last)):
                    step(t)

        return steps_of, finish, sent

    q_steps, q_finish, q_sent = two_way(
        q_term, qfsend, qfrecv, qf_send, qf_recv, qbsend, qbrecv, qb_send, qb_recv)
    k_steps, k_finish, k_sent = two_way(
        k_term, kfsend, kfrecv, kf_send, kf_recv, kbsend, kbrecv, kb_send, kb_recv)

    def weight_part(k):
        for c in range(D // 256):
            piece = dot(xf[:, c * 256:(c + 1) * 256], gqk[:, k * width:(k + 1) * width], 0, 0)
            if fused:
                gpart[k, c * 256:(c + 1) * 256] = piece.astype(BF16)
            else:
                wg_ref[c * 256:(c + 1) * 256, k * width:(k + 1) * width] = piece

    for p in range(n_pairs):
        for d in range(1, n_fam):
            t_wait(1, p, d)
        spread(dot(tfull[1, p], qs[p], 0, 0), gqk, width + p * 128)
    weight_part(1)
    k_steps(0, 1)
    for p in range(n_pairs):
        spread(dot(both(1, p), ks[p]), gqk, p * 128)
    weight_part(0)
    order = []
    for k in range(n_seq):
        order += [k // 2 if k % 2 == 0 else n_seq - 1 - k // 2]
    if fused:
        for to_z in order:
            for d in range(1, n_fam):
                gx_copy(to_z, d).start()

    for p in range(n_pairs):
        for d in range(1, n_fam):
            t_wait(0, p, d)
        mixed = dot(both(0, p), vs[p])
        for r in range(rows):
            mf[r * cols:(r + 1) * cols, pl.ds(pl.multiple_of(h * width + p * 128, 128), 128)] = (
                mixed[:, r * 128:(r + 1) * 128].astype(BF16))
    cm = to_head(mf.at[:, mine], mf.at[:, mine], 3)
    cm.start()
    k_steps(1, 2)
    for p in range(n_pairs):
        spread(dot(tfull[0, p], os_[p], 0, 0), gv, p * 128)

    def back(at):
        return (dot(gqk[:, 0:width], wq_ref[at, :], 1, 1)
                + dot(gqk[:, width:2 * width], wk_ref[at, :], 1, 1)
                + dot(gv[...], wv_ref[at, :], 1, 1))

    q_steps(0, 1)
    igs[...] = back(theirs).astype(igs.dtype)
    ci = to_head(igs, igr, 4)
    ci.start()
    k_steps(2, last)
    q_steps(1, 2)
    if fused:
        summed = k_finish()
        kxsend[...] = summed.astype(BF16).reshape(n_fam, own_rows, width)
        for d in range(1, n_fam):
            kx_copy(d).start()
    cm.wait()
    out_ref[...] = dot(mf[...], wo_ref[...]).astype(BF16)
    q_steps(2, last)
    mine_grad = back(mine)
    ci.wait()
    ig_ref[...] = (mine_grad + igr[...].astype(F32)).astype(BF16)
    if fused:
        wg_ref[:, 0, :] = q_finish()
        total = kxsend[x].astype(F32)
        for d in range(1, n_fam):
            kx_copy(d).wait_recv()
            total = total + kxrecv[d].astype(F32)
        wg_ref[:, 1, :] = total
        q_sent()
        k_sent()
        for d in range(1, n_fam):
            kx_copy(d).wait_send()
        for to_z in order:
            for d in range(1, n_fam):
                gx_copy(to_z, d).wait_send()

    for s in range(steps):
        for d in range(1, n_fam):
            x_copy(s, d).wait_send()

        @pl.when(z < last)
        def _():
            f_copy(s).wait_send()

        @pl.when(z > 0)
        def _():
            b_copy(s).wait_send()
    for k in range(2):
        for p in range(n_pairs):
            for d in range(1, n_fam):
                t_copy(k, p, d).wait_send()


def shards(cfg, blocks, cotangent, w_query, w_key, w_value, w_out, block_family, family_depth):
    n_seq, n_fam, rows, cols, own_rows, fused = cfg
    tokens = rows * cols
    width = blocks.shape[3]
    n_pairs = width // 128
    steps = 2 * n_pairs
    chunk = 256 // n_fam
    lanes = rows * 128
    vmem = pltpu.VMEM
    dma = pltpu.SemaphoreType.DMA
    g_z, g_r = (n_seq, own_rows) if fused else (1, 16)
    g_all = D if fused else 16
    scratch = [
        vmem((tokens, D), BF16), vmem((tokens, D), BF16), vmem((width, D), BF16),
        vmem((tokens, D), BF16), vmem((tokens, width), BF16), vmem((tokens, width), BF16),
        vmem((n_pairs, 256, lanes), BF16), vmem((n_pairs, 256, lanes), BF16),
        vmem((n_pairs, 256, lanes), BF16), vmem((n_pairs, 256, lanes), BF16),
        vmem((n_pairs, 128, lanes), BF16), vmem((n_pairs, 128, lanes), BF16),
        vmem((tokens, 2 * width), BF16), vmem((tokens, width), BF16),
        vmem((steps, 256, 128), F32), vmem((steps, n_fam, chunk, 128), F32),
        vmem((steps, chunk, 128), F32), vmem((steps, chunk, 128), F32),
        vmem((steps, chunk, 128), F32), vmem((steps, chunk, 128), F32),
        vmem((2, n_pairs, n_fam, chunk, 128), BF16), vmem((2, n_pairs, 256, 128), BF16),
        vmem((n_pairs, n_fam, chunk, 128), F32),
        vmem((2, g_all, width), BF16), vmem((g_z, n_fam, g_r, width), BF16),
        vmem((g_z, g_r, width), BF16), vmem((g_z, g_r, width), BF16),
        vmem((g_z, g_r, width), BF16), vmem((g_z, g_r, width), BF16),
        vmem((g_z, n_fam * g_r, width), BF16), vmem((g_z, n_fam * g_r, width), BF16),
        vmem((g_z, n_fam * g_r, width), BF16), vmem((g_z, n_fam * g_r, width), BF16),
        vmem((n_fam, g_r, width), BF16), vmem((n_fam, g_r, width), BF16),
        dma((5,)), dma((5,)), dma((steps, n_fam)), dma((steps, n_fam)),
        dma((steps,)), dma((steps,)), dma((steps,)), dma((steps,)),
        dma((2, n_pairs, n_fam)), dma((2, n_pairs, n_fam)),
        dma((g_z, n_fam)), dma((g_z, n_fam)), dma((g_z,)), dma((g_z,)), dma((g_z,)), dma((g_z,)),
        dma((g_z,)), dma((g_z,)), dma((g_z,)), dma((g_z,)), dma((n_fam,)), dma((n_fam,)),
    ]
    spec = pl.BlockSpec(memory_space=pltpu.VMEM)
    smem = pl.BlockSpec(memory_space=pltpu.SMEM)
    layer_out, input_grad, weight_grad = pl.pallas_call(
        functools.partial(kernel, cfg),
        out_shape=(
            jax.ShapeDtypeStruct((tokens, width), BF16),
            jax.ShapeDtypeStruct((tokens, width), BF16),
            jax.ShapeDtypeStruct((own_rows, 2, width) if fused else (D, 2 * width), F32),
        ),
        in_specs=[smem, smem] + [spec] * 6,
        out_specs=(spec, spec, spec),
        scratch_shapes=scratch,
        compiler_params=pltpu.CompilerParams(
            collective_id=0, has_side_effects=True, vmem_limit_bytes=56 * 1024 * 1024),
    )(block_family, family_depth, blocks.reshape(tokens, width), cotangent.reshape(tokens, width),
      w_query, w_key, w_value, w_out)
    if not fused:
        weight_grad = lax.psum_scatter(weight_grad, ("seq", "fam"), scatter_dimension=0, tiled=True)
    return (
        layer_out.reshape(blocks.shape),
        input_grad.reshape(blocks.shape),
        weight_grad.reshape(own_rows, 2, width),
    )


def solution(mesh):
    n_seq, n_fam = mesh.shape["seq"], mesh.shape["fam"]

    def local(*arrays):
        own_rows = D // (n_seq * n_fam)
        blocks = arrays[0]
        rows = blocks.shape[0] * blocks.shape[1]
        cfg = (n_seq, n_fam, rows, blocks.shape[2], own_rows, own_rows % 16 == 0)
        return shards(cfg, *arrays)

    token_spec = P(("groups", "seq", "fam"), None, None, "head")
    weight_spec = P(None, "head")
    return jax.shard_map(
        local,
        mesh=mesh,
        in_specs=(token_spec, token_spec, weight_spec, weight_spec, weight_spec, weight_spec,
                  P("groups"), P("groups")),
        out_specs=(token_spec, token_spec, P(("groups", "seq", "fam"), None, "head")),
        check_vma=False,
    )
```

```python
import functools

import jax
import jax.numpy as jnp
from jax import lax
from jax.experimental import pallas as pl
from jax.experimental.pallas import tpu as pltpu
from jax.sharding import PartitionSpec as P

D = 768
H = 12
MESH = pl.DeviceIdType.MESH
F32 = jnp.float32
BF16 = jnp.bfloat16


def dot(a, b, ca=1, cb=0):
    return lax.dot_general(a, b, (((ca,), (cb,)), ((), ())), preferred_element_type=F32)


def kernel(cfg, fam_ref, depth_ref, x_ref, cot_ref, wq_ref, wk_ref, wv_ref, wo_ref,
           out_ref, ig_ref, wg_ref,
           xf, cf, wor, mf, igr, igs, qs, ks, vs, os_, kp, vp, gqk, gv,
           part, xrecv, lrecv, rrecv, fsend, bsend, tsend, tfull, att, gpart, gxrecv,
           qfrecv, qbrecv, qfsend, qbsend, kfrecv, kbrecv, kfsend, kbsend, kxsend, kxrecv,
           h_send, h_recv, x_send, x_recv, f_send, f_recv, b_send, b_recv, t_send, t_recv,
           gx_send, gx_recv, qf_send, qf_recv, qb_send, qb_recv,
           kf_send, kf_recv, kb_send, kb_recv, kx_send, kx_recv):
    n_seq, n_fam, rows, cols, own_rows, fused = cfg
    width = x_ref.shape[1]
    n_pairs = width // 128
    head_size = D // H
    chunk = 256 // n_fam
    n_blocks = n_seq * n_fam
    steps = 2 * n_pairs
    z = lax.axis_index("seq")
    x = lax.axis_index("fam")
    h = lax.axis_index("head")
    other = 1 - h
    last = n_seq - 1

    def fam_at(d):
        return lax.rem(x + d + n_fam, n_fam)

    barrier = pltpu.get_barrier_semaphore()
    pl.semaphore_signal(barrier, inc=1, device_id={"head": other}, device_id_type=MESH)
    for d in range(1, n_fam):
        pl.semaphore_signal(barrier, inc=1, device_id={"fam": fam_at(d)}, device_id_type=MESH)

    @pl.when(z > 0)
    def _():
        pl.semaphore_signal(barrier, inc=1, device_id={"seq": z - 1}, device_id_type=MESH)

    @pl.when(z < last)
    def _():
        pl.semaphore_signal(barrier, inc=1, device_id={"seq": z + 1}, device_id_type=MESH)

    @pl.when(z == 0)
    def _():
        lrecv[...] = jnp.zeros_like(lrecv)
        if fused:
            qfrecv[...] = jnp.zeros_like(qfrecv)
            kfrecv[...] = jnp.zeros_like(kfrecv)

    @pl.when(z == last)
    def _():
        rrecv[...] = jnp.zeros_like(rrecv)
        if fused:
            qbrecv[...] = jnp.zeros_like(qbrecv)
            kbrecv[...] = jnp.zeros_like(kbrecv)

    pl.semaphore_wait(barrier, n_fam + jnp.where(z > 0, 1, 0) + jnp.where(z < last, 1, 0))

    mine = pl.ds(pl.multiple_of(h * width, 128), width)
    theirs = pl.ds(pl.multiple_of(other * width, 128), width)

    def to_head(src, dst, k):
        return pltpu.make_async_remote_copy(
            src_ref=src, dst_ref=dst, send_sem=h_send.at[k], recv_sem=h_recv.at[k],
            device_id={"head": other}, device_id_type=MESH)

    cx = to_head(x_ref, xf.at[:, mine], 0)
    cx.start()
    cc = to_head(cot_ref, cf.at[:, mine], 1)
    cc.start()
    cw = to_head(wo_ref.at[theirs, :], wor.at[:, mine], 2)
    cw.start()
    xf[:, mine] = x_ref[...]
    cf[:, mine] = cot_ref[...]
    wor[:, mine] = wo_ref[mine, :]

    base = z * n_fam

    def family(b):
        return fam_ref[b]

    def same(a, b):
        return jnp.where(a == b, 1.0, 0.0).astype(F32)

    f_rel = [family(base + fam_at(d)) for d in range(n_fam)]
    f_neg = [family(base + fam_at(-d)) for d in range(n_fam)]
    f_first = family(base)
    f_last = family(base + n_fam - 1)
    has_left = jnp.where(z > 0, 1.0, 0.0).astype(F32)
    has_right = jnp.where(z < last, 1.0, 0.0).astype(F32)
    f_prev = family(base - jnp.where(z > 0, 1, 0))
    f_next = family(base + n_fam - 1 + jnp.where(z < last, 1, 0))
    my_family = f_rel[0]
    first = lax.fori_loop(
        0, n_blocks, lambda b, c: c + jnp.where(fam_ref[b] < my_family, 1, 0), jnp.int32(0))
    my_depth = depth_ref[my_family]
    rank = base + x - first
    live = [jnp.where(rank * rows + r < my_depth, 1.0, 0.0).astype(F32) for r in range(rows)]
    scale = []
    for d in range(n_fam):
        deep = jnp.full((8, 128), depth_ref[f_rel[d]].astype(F32), F32)
        scale.append((1.0 / (jnp.sqrt(jnp.full((8, 128), float(head_size), F32)) * jnp.sqrt(deep)))[0:1])

    low = lax.broadcasted_iota(jnp.int32, (cols, 128), 1) < head_size

    def keep(value, stack, plain, masked):
        for r in range(rows):
            for p in range(n_pairs):
                v = value[r * cols:(r + 1) * cols, p * 128:(p + 1) * 128]
                v = v.astype(BF16).astype(F32)
                if masked:
                    v = v * live[r]
                lanes = slice(r * 128, (r + 1) * 128)
                stack[p, 0:cols, lanes] = jnp.where(low, v, 0.0).astype(BF16)
                stack[p, cols:2 * cols, lanes] = jnp.where(low, 0.0, v).astype(BF16)
                if plain is not None:
                    plain[p, :, lanes] = v.astype(BF16)

    def x_copy(s, d):
        to = fam_at(d)
        return pltpu.make_async_remote_copy(
            src_ref=part.at[s, pl.ds(pl.multiple_of(to * chunk, 16), chunk)],
            dst_ref=xrecv.at[s, d], send_sem=x_send.at[s, d], recv_sem=x_recv.at[s, d],
            device_id={"fam": to}, device_id_type=MESH)

    cx.wait()
    keep(dot(xf[...], wq_ref[...]), qs, None, True)
    keep(dot(xf[...], wk_ref[...]), ks, kp, True)
    for p in range(n_pairs):
        part[p] = dot(qs[p], kp[p], 1, 1)
        for d in range(1, n_fam):
            x_copy(p, d).start()
    keep(dot(xf[...], wv_ref[...]), vs, vp, False)
    cc.wait()
    cw.wait()
    keep(dot(cf[...], wor[...], 1, 1), os_, None, False)
    for p in range(n_pairs):
        part[n_pairs + p] = dot(os_[p], vp[p], 1, 1)
        for d in range(1, n_fam):
            x_copy(n_pairs + p, d).start()

    own = pl.ds(pl.multiple_of(x * chunk, 16), chunk)

    def f_copy(s):
        return pltpu.make_async_remote_copy(
            src_ref=fsend.at[s], dst_ref=lrecv.at[s], send_sem=f_send.at[s], recv_sem=f_recv.at[s],
            device_id={"seq": z + 1}, device_id_type=MESH)

    def b_copy(s):
        return pltpu.make_async_remote_copy(
            src_ref=bsend.at[s], dst_ref=rrecv.at[s], send_sem=b_send.at[s], recv_sem=b_recv.at[s],
            device_id={"seq": z - 1}, device_id_type=MESH)

    def row_terms(s):
        return [part[s, own]] + [xrecv[s, d] for d in range(1, n_fam)]

    def chain(t, carry):
        sf = t - z
        sb = t - (last - z)

        @pl.when((sf >= 0) & (sf < steps))
        def _():
            @pl.when(z <= last - z)
            def _():
                for d in range(1, n_fam):
                    x_copy(sf, d).wait_recv()

            @pl.when(z > 0)
            def _():
                f_copy(sf).wait_recv()

            @pl.when(z < last)
            def _():
                total = (has_left * same(f_prev, f_last)) * lrecv[sf]
                for d, term in enumerate(row_terms(sf)):
                    total = total + same(f_neg[d], f_last) * term
                fsend[sf] = total
                f_copy(sf).start()

        @pl.when((sb >= 0) & (sb < steps))
        def _():
            @pl.when(z > last - z)
            def _():
                for d in range(1, n_fam):
                    x_copy(sb, d).wait_recv()

            @pl.when(z < last)
            def _():
                b_copy(sb).wait_recv()

            @pl.when(z > 0)
            def _():
                total = (has_right * same(f_next, f_first)) * rrecv[sb]
                for d, term in enumerate(row_terms(sb)):
                    total = total + same(f_neg[d], f_first) * term
                bsend[sb] = total
                b_copy(sb).start()

        return carry

    logits_done = n_pairs + last
    lax.fori_loop(0, logits_done, chain, jnp.int32(0))

    def t_copy(k, p, d):
        return pltpu.make_async_remote_copy(
            src_ref=tsend.at[k, p, d], dst_ref=tfull.at[k, p, own],
            send_sem=t_send.at[k, p, d], recv_sem=t_recv.at[k, p, d],
            device_id={"fam": fam_at(d)}, device_id_type=MESH)

    def t_wait(k, p, d):
        came = pl.ds(pl.multiple_of(fam_at(-d) * chunk, 16), chunk)
        pltpu.make_async_remote_copy(
            src_ref=tsend.at[k, p, d], dst_ref=tfull.at[k, p, came],
            send_sem=t_send.at[k, p, d], recv_sem=t_recv.at[k, p, d],
            device_id={"fam": fam_at(d)}, device_id_type=MESH).wait_recv()

    def totals(s):
        terms = row_terms(s)
        left, right = lrecv[s], rrecv[s]
        sums = []
        for e in range(n_fam):
            total = (has_left * same(f_prev, f_rel[e])) * left
            total = total + (has_right * same(f_next, f_rel[e])) * right
            for d in range(n_fam):
                total = total + same(f_neg[d], f_rel[e]) * terms[d]
            sums.append(total)
        return sums

    def give(k, p, e, value):
        if e == 0:
            tfull[k, p, own] = value
        else:
            tsend[k, p, e] = value
            t_copy(k, p, e).start()

    for p in range(n_pairs):
        sums = totals(p)
        for e in list(range(1, n_fam)) + [0]:
            expo = jnp.exp(sums[e] * scale[e])
            attention = expo / jnp.sum(expo, axis=-1, keepdims=True)
            att[p, e] = attention
            give(0, p, e, attention.astype(BF16))
        if p < last:
            chain(logits_done + p, 0)
    for t in range(logits_done + min(n_pairs, last), steps + last):
        chain(t, 0)

    for p in range(n_pairs):
        sums = totals(n_pairs + p)
        for e in list(range(1, n_fam)) + [0]:
            attention, grad = att[p, e], sums[e]
            centred = grad - jnp.sum(attention * grad, axis=-1, keepdims=True)
            give(1, p, e, (scale[e] * attention * centred).astype(BF16))

    def both(k, p):
        return jnp.concatenate([tfull[k, p, 0:cols], tfull[k, p, cols:2 * cols]], axis=1)

    def spread(value, ref, at):
        for r in range(rows):
            ref[r * cols:(r + 1) * cols, at:at + 128] = value[:, r * 128:(r + 1) * 128].astype(BF16)

    def part_rows(to_z, to_x, count):
        return pl.ds(pl.multiple_of((to_z * n_fam + to_x) * own_rows, 16), count)

    def gx_copy(to_z, d):
        return pltpu.make_async_remote_copy(
            src_ref=gpart.at[0, part_rows(to_z, fam_at(d), own_rows)], dst_ref=gxrecv.at[to_z, d],
            send_sem=gx_send.at[to_z, d], recv_sem=gx_recv.at[to_z, d],
            device_id={"fam": fam_at(d)}, device_id_type=MESH)

    def kx_copy(d):
        return pltpu.make_async_remote_copy(
            src_ref=kxsend.at[fam_at(d)], dst_ref=kxrecv.at[d], send_sem=kx_send.at[d], recv_sem=kx_recv.at[d],
            device_id={"fam": fam_at(d)}, device_id_type=MESH)

    def q_term(to_z):
        total = gpart[0, part_rows(to_z, x, own_rows)].astype(F32)
        for d in range(1, n_fam):
            gx_copy(to_z, d).wait_recv()
            total = total + gxrecv[to_z, d].astype(F32)
        return total

    def k_term(to_z):
        return gpart[1, part_rows(to_z, 0, n_fam * own_rows)].astype(F32)

    def two_way(term, fsrc, fdst, fs, fr, bsrc, bdst, bs, br):
        def fcopy(to_z):
            return pltpu.make_async_remote_copy(
                src_ref=fsrc.at[to_z], dst_ref=fdst.at[to_z], send_sem=fs.at[to_z], recv_sem=fr.at[to_z],
                device_id={"seq": z + 1}, device_id_type=MESH)

        def bcopy(to_z):
            return pltpu.make_async_remote_copy(
                src_ref=bsrc.at[to_z], dst_ref=bdst.at[to_z], send_sem=bs.at[to_z], recv_sem=br.at[to_z],
                device_id={"seq": z - 1}, device_id_type=MESH)

        def step(t):
            @pl.when(t >= z)
            def _():
                to_z = last - (t - z)
                total = term(to_z)

                @pl.when(z > 0)
                def _():
                    fcopy(to_z).wait_recv()

                fsrc[to_z] = (total + fdst[to_z].astype(F32)).astype(BF16)
                fcopy(to_z).start()

            @pl.when(t >= last - z)
            def _():
                to_z = t - (last - z)
                total = term(to_z)

                @pl.when(z < last)
                def _():
                    bcopy(to_z).wait_recv()

                bsrc[to_z] = (total + bdst[to_z].astype(F32)).astype(BF16)
                bcopy(to_z).start()

        def finish():
            total = term(z)

            @pl.when(z > 0)
            def _():
                fcopy(z).wait_recv()

            @pl.when(z < last)
            def _():
                bcopy(z).wait_recv()

            return total + fdst[z].astype(F32) + bdst[z].astype(F32)

        def sent():
            for t in range(last):
                @pl.when(t >= z)
                def _():
                    fcopy(last - (t - z)).wait_send()

                @pl.when(t >= last - z)
                def _():
                    bcopy(t - (last - z)).wait_send()

        def steps_of(lo, hi):
            if fused:
                for t in range(lo, min(hi, last)):
                    step(t)

        return steps_of, finish, sent

    q_steps, q_finish, q_sent = two_way(
        q_term, qfsend, qfrecv, qf_send, qf_recv, qbsend, qbrecv, qb_send, qb_recv)
    k_steps, k_finish, k_sent = two_way(
        k_term, kfsend, kfrecv, kf_send, kf_recv, kbsend, kbrecv, kb_send, kb_recv)

    def weight_part(k):
        for c in range(D // 256):
            piece = dot(xf[:, c * 256:(c + 1) * 256], gqk[:, k * width:(k + 1) * width], 0, 0)
            if fused:
                gpart[k, c * 256:(c + 1) * 256] = piece.astype(BF16)
            else:
                wg_ref[c * 256:(c + 1) * 256, k * width:(k + 1) * width] = piece

    for p in range(n_pairs):
        for d in range(1, n_fam):
            t_wait(0, p, d)
        mixed = dot(both(0, p), vs[p])
        for r in range(rows):
            mf[r * cols:(r + 1) * cols, pl.ds(pl.multiple_of(h * width + p * 128, 128), 128)] = (
                mixed[:, r * 128:(r + 1) * 128].astype(BF16))
    cm = to_head(mf.at[:, mine], mf.at[:, mine], 3)
    cm.start()

    for p in range(n_pairs):
        for d in range(1, n_fam):
            t_wait(1, p, d)
        spread(dot(tfull[1, p], qs[p], 0, 0), gqk, width + p * 128)
    weight_part(1)
    k_steps(0, 1)
    for p in range(n_pairs):
        spread(dot(both(1, p), ks[p]), gqk, p * 128)
    weight_part(0)
    order = []
    for k in range(n_seq):
        order += [k // 2 if k % 2 == 0 else n_seq - 1 - k // 2]
    if fused:
        for to_z in order:
            for d in range(1, n_fam):
                gx_copy(to_z, d).start()

    k_steps(1, 2)
    for p in range(n_pairs):
        spread(dot(tfull[0, p], os_[p], 0, 0), gv, p * 128)

    def back(at):
        return (dot(gqk[:, 0:width], wq_ref[at, :], 1, 1)
                + dot(gqk[:, width:2 * width], wk_ref[at, :], 1, 1)
                + dot(gv[...], wv_ref[at, :], 1, 1))

    q_steps(0, 1)
    igs[...] = back(theirs).astype(igs.dtype)
    ci = to_head(igs, igr, 4)
    ci.start()
    k_steps(2, last)
    q_steps(1, 2)
    if fused:
        summed = k_finish()
        kxsend[...] = summed.astype(BF16).reshape(n_fam, own_rows, width)
        for d in range(1, n_fam):
            kx_copy(d).start()
    cm.wait()
    out_ref[...] = dot(mf[...], wo_ref[...]).astype(BF16)
    q_steps(2, last)
    mine_grad = back(mine)
    ci.wait()
    ig_ref[...] = (mine_grad + igr[...].astype(F32)).astype(BF16)
    if fused:
        wg_ref[:, 0, :] = q_finish()
        total = kxsend[x].astype(F32)
        for d in range(1, n_fam):
            kx_copy(d).wait_recv()
            total = total + kxrecv[d].astype(F32)
        wg_ref[:, 1, :] = total
        q_sent()
        k_sent()
        for d in range(1, n_fam):
            kx_copy(d).wait_send()
        for to_z in order:
            for d in range(1, n_fam):
                gx_copy(to_z, d).wait_send()

    for s in range(steps):
        for d in range(1, n_fam):
            x_copy(s, d).wait_send()

        @pl.when(z < last)
        def _():
            f_copy(s).wait_send()

        @pl.when(z > 0)
        def _():
            b_copy(s).wait_send()
    for k in range(2):
        for p in range(n_pairs):
            for d in range(1, n_fam):
                t_copy(k, p, d).wait_send()


def shards(cfg, blocks, cotangent, w_query, w_key, w_value, w_out, block_family, family_depth):
    n_seq, n_fam, rows, cols, own_rows, fused = cfg
    tokens = rows * cols
    width = blocks.shape[3]
    n_pairs = width // 128
    steps = 2 * n_pairs
    chunk = 256 // n_fam
    lanes = rows * 128
    vmem = pltpu.VMEM
    dma = pltpu.SemaphoreType.DMA
    g_z, g_r = (n_seq, own_rows) if fused else (1, 16)
    g_all = D if fused else 16
    scratch = [
        vmem((tokens, D), BF16), vmem((tokens, D), BF16), vmem((width, D), BF16),
        vmem((tokens, D), BF16), vmem((tokens, width), BF16), vmem((tokens, width), BF16),
        vmem((n_pairs, 256, lanes), BF16), vmem((n_pairs, 256, lanes), BF16),
        vmem((n_pairs, 256, lanes), BF16), vmem((n_pairs, 256, lanes), BF16),
        vmem((n_pairs, 128, lanes), BF16), vmem((n_pairs, 128, lanes), BF16),
        vmem((tokens, 2 * width), BF16), vmem((tokens, width), BF16),
        vmem((steps, 256, 128), F32), vmem((steps, n_fam, chunk, 128), F32),
        vmem((steps, chunk, 128), F32), vmem((steps, chunk, 128), F32),
        vmem((steps, chunk, 128), F32), vmem((steps, chunk, 128), F32),
        vmem((2, n_pairs, n_fam, chunk, 128), BF16), vmem((2, n_pairs, 256, 128), BF16),
        vmem((n_pairs, n_fam, chunk, 128), F32),
        vmem((2, g_all, width), BF16), vmem((g_z, n_fam, g_r, width), BF16),
        vmem((g_z, g_r, width), BF16), vmem((g_z, g_r, width), BF16),
        vmem((g_z, g_r, width), BF16), vmem((g_z, g_r, width), BF16),
        vmem((g_z, n_fam * g_r, width), BF16), vmem((g_z, n_fam * g_r, width), BF16),
        vmem((g_z, n_fam * g_r, width), BF16), vmem((g_z, n_fam * g_r, width), BF16),
        vmem((n_fam, g_r, width), BF16), vmem((n_fam, g_r, width), BF16),
        dma((5,)), dma((5,)), dma((steps, n_fam)), dma((steps, n_fam)),
        dma((steps,)), dma((steps,)), dma((steps,)), dma((steps,)),
        dma((2, n_pairs, n_fam)), dma((2, n_pairs, n_fam)),
        dma((g_z, n_fam)), dma((g_z, n_fam)), dma((g_z,)), dma((g_z,)), dma((g_z,)), dma((g_z,)),
        dma((g_z,)), dma((g_z,)), dma((g_z,)), dma((g_z,)), dma((n_fam,)), dma((n_fam,)),
    ]
    spec = pl.BlockSpec(memory_space=pltpu.VMEM)
    smem = pl.BlockSpec(memory_space=pltpu.SMEM)
    layer_out, input_grad, weight_grad = pl.pallas_call(
        functools.partial(kernel, cfg),
        out_shape=(
            jax.ShapeDtypeStruct((tokens, width), BF16),
            jax.ShapeDtypeStruct((tokens, width), BF16),
            jax.ShapeDtypeStruct((own_rows, 2, width) if fused else (D, 2 * width), F32),
        ),
        in_specs=[smem, smem] + [spec] * 6,
        out_specs=(spec, spec, spec),
        scratch_shapes=scratch,
        compiler_params=pltpu.CompilerParams(
            collective_id=0, has_side_effects=True, vmem_limit_bytes=56 * 1024 * 1024),
    )(block_family, family_depth, blocks.reshape(tokens, width), cotangent.reshape(tokens, width),
      w_query, w_key, w_value, w_out)
    if not fused:
        weight_grad = lax.psum_scatter(weight_grad, ("seq", "fam"), scatter_dimension=0, tiled=True)
    return (
        layer_out.reshape(blocks.shape),
        input_grad.reshape(blocks.shape),
        weight_grad.reshape(own_rows, 2, width),
    )


def solution(mesh):
    n_seq, n_fam = mesh.shape["seq"], mesh.shape["fam"]

    def local(*arrays):
        own_rows = D // (n_seq * n_fam)
        blocks = arrays[0]
        rows = blocks.shape[0] * blocks.shape[1]
        cfg = (n_seq, n_fam, rows, blocks.shape[2], own_rows, own_rows % 16 == 0)
        return shards(cfg, *arrays)

    token_spec = P(("groups", "seq", "fam"), None, None, "head")
    weight_spec = P(None, "head")
    return jax.shard_map(
        local,
        mesh=mesh,
        in_specs=(token_spec, token_spec, weight_spec, weight_spec, weight_spec, weight_spec,
                  P("groups"), P("groups")),
        out_specs=(token_spec, token_spec, P(("groups", "seq", "fam"), None, "head")),
        check_vma=False,
    )
```
